32 devices in a mesh: groups: 2 (over y), dp: 4 (over z), ctx: 4 (over x, core).
Axes of the slice: x: 2, y: 2, z: 4, core: 2. Of those that a mesh axis runs over, the one named last changes fastest.
Arguments:
- queries: bfloat16 [8, 1024, 2048], P(('groups', 'dp'), 'ctx'), parts along dimension 0, may hold values from -480 to 480
- keys: bfloat16 [8, 1024, 256], P(('groups', 'dp'), 'ctx'), parts along dimension 0, may hold values from -4.1 to 4.1
- values: bfloat16 [8, 1024, 256], P(('groups', 'dp'), 'ctx'), parts along dimension 0, may hold values from -6 to 6
- grad_out: bfloat16 [8, 1024, 2048], P(('groups', 'dp'), 'ctx'), parts along dimension 0, may hold values from -6 to 6
- sinks: float32 [32], replicated, may hold values from 0 to 6
- doc_ids: int32 [8, 1024], P(('groups', 'dp')), parts along dimension 0, may hold values from 0 to 1, never falling along the last dimension, each value on 1 to 768 neighbouring positions
- swap_flags: int32 [8, 4, 16], P(('groups', 'dp'), 'ctx'), parts along dimension 0, may hold values from 0 to 1, as said below
Outputs:
- attn_out: bfloat16 [8, 1024, 2048], P(('groups', 'dp'), 'ctx'), parts along dimension 0
- grad_queries: bfloat16 [8, 1024, 2048], P(('groups', 'dp'), 'ctx'), parts along dimension 0
- grad_keys: bfloat16 [8, 1024, 256], P(('groups', 'dp'), 'ctx'), parts along dimension 0
- grad_values: bfloat16 [8, 1024, 256], P(('groups', 'dp'), 'ctx'), parts along dimension 0
The draws below stay inside these ranges and needn't reach their ends.
There are 2 independent parts, one for each index of `groups`. The reference program is written for one: setup_inputs(seed, part) draws one part's arguments, and reference() takes and returns one part's arrays. A program takes and returns all parts, laid end to end along the dimension named above; an argument that names none is the same for every part. Nothing has to cross between parts.
Inputs may be any that keep to these rules, and one draw needn't show every extreme that they name: `doc_ids`: each of the 2 responses of a pack covers between 256 and 768 neighbouring positions. swap_flags of rank i and run c equal those of its partner rank (i + 2) mod 4 and run c; each device has at most 1 ones, and some device has exactly 1.
All inputs are finite; a program needn't handle non-finite values.
Results may differ from the reference program's by a relative error of at most 0.019.
Values may be sent and summed in bfloat16 or wider, within the bound.
A program may use at most 64 MiB of HBM per device.

```python
import math
import jax
import jax.numpy as jnp
import numpy as np
from jax import lax

QUERY_HEADS = 32
KEY_VALUE_HEADS = 4
HEAD_SIZE = 64
WINDOW = 128
BLK = 16
CAP = 1
SEQS = 2
BLOCKS = 16
ROWS = 256
BATCH_PACKS = 4
STRETCHES = 4
PACK_TOKENS = 1024
DOC_MOST = 768


def draw_queries(key, part):
    leading_key = jax.random.fold_in(jax.random.fold_in(key, 11), 0)
    start_offset = jnp.clip(jax.random.normal(leading_key, (BATCH_PACKS, PACK_TOKENS, QUERY_HEADS * HEAD_SIZE), jnp.float32), -4.0, 4.0)
    return start_offset.astype(jnp.bfloat16)


def draw_keys(key, part):
    leading_key = jax.random.fold_in(jax.random.fold_in(key, 23), 0)
    start_offset = jnp.clip(jax.random.normal(leading_key, (BATCH_PACKS, PACK_TOKENS, KEY_VALUE_HEADS * HEAD_SIZE), jnp.float32), -4.0, 4.0)
    return start_offset.astype(jnp.bfloat16)


def draw_swap_flags(key, part):
    count_key, order_key, pair_key, run_key = jax.random.split(jax.random.fold_in(key, 37), 4)
    half_packs = BATCH_PACKS // 2
    counts = jax.random.randint(count_key, (half_packs, STRETCHES), 0, CAP + 1)
    full_pair = jax.random.randint(pair_key, (), 0, half_packs)
    full_run = jax.random.randint(run_key, (), 0, STRETCHES)
    counts = counts.at[full_pair, full_run].set(CAP)
    noise_bits = jax.random.randint(order_key, (half_packs, STRETCHES, BLOCKS), 0, 1 << 20)
    distinct = noise_bits * BLOCKS + jnp.arange(BLOCKS, dtype=jnp.int32)[None, None, :]
    ranking = jnp.argsort(jnp.argsort(distinct, axis=-1), axis=-1)
    lower_half = (ranking < counts[:, :, None]).astype(jnp.int32)
    return jnp.concatenate([lower_half, lower_half], axis=0)


def shard_levels(rng, shape, cuts, least, largest):
    gain, own = 1.0, jax.random.fold_in(rng, 6)
    for position, blocks in cuts:
        steps = jnp.exp(jax.random.uniform(jax.random.fold_in(own, position), (blocks,), jnp.float32, least / len(cuts), largest / len(cuts)))
        gain = gain * jnp.repeat(steps, shape[position] // blocks).reshape([-1 if axis == position else 1 for axis in range(len(shape))])
    return gain


def split_up(amount, total, limit, slope):
    weights = [(1 << 20) // math.isqrt(standing ** slope) + 1 for standing in range(2, amount + 1)]
    surplus, holding = total - limit - (amount - 1), [1] * (amount - 1)
    while surplus > 0:
        candidates = [i for i in range(amount - 1) if holding[i] < limit]
        whole, left = sum([weights[i] for i in candidates]), surplus
        for i in candidates:
            extra = min(limit - holding[i], max(1, left * weights[i] // whole), surplus)
            holding[i] = holding[i] + extra
            surplus = surplus - extra
    return np.array([limit] + holding)


def ragged(key, count, total, bound, slope):
    if count == 2:
        one = jax.random.randint(key, (), max(1, total - bound), min(bound, total - 1) + 1)
        return jnp.stack([one, total - one])
    tallies = jnp.asarray(split_up(count, total, bound, slope), jnp.int32)
    couples = (count - 1) // 2
    donor, taker = tallies[1:1 + 2 * couples:2], tallies[2:2 + 2 * couples:2]
    slack = jnp.minimum(donor - 1, bound - taker)
    moved = jax.random.randint(jax.random.fold_in(key, 1), (couples,), 0, 1 << 20) % (slack + 1)
    tallies = tallies.at[1:1 + 2 * couples:2].set(donor - moved).at[2:2 + 2 * couples:2].set(taker + moved)
    return tallies[jax.random.permutation(jax.random.fold_in(key, 2), count)]


def centred(rng, dims, scale, most, shards=(), held_as=jnp.bfloat16):
    drawn = jax.random.normal(rng, dims, jnp.float32) * scale
    if len(shards) > 0:
        drawn = shard_levels(rng, dims, shards, -0.22, 0.18) * drawn
    return jnp.clip(drawn, min=-most, max=most).astype(held_as)


def setup_inputs(seed: int = 0, part: int = 0) -> dict:
    arg_keys = jax.random.split(jax.random.key(seed), 8)
    own_keys = jax.random.split(jax.random.fold_in(arg_keys[7], part), 8)
    queries = draw_queries(jax.random.fold_in(jax.random.fold_in(arg_keys[7], part), 71), part)
    keys = draw_keys(jax.random.fold_in(jax.random.fold_in(arg_keys[7], part), 71), part)
    values = centred(own_keys[2], (BATCH_PACKS, PACK_TOKENS, KEY_VALUE_HEADS * HEAD_SIZE), 1.0, 6.0, ((0, 4), (1, 4)))
    grad_out = centred(own_keys[3], (BATCH_PACKS, PACK_TOKENS, QUERY_HEADS * HEAD_SIZE), 1.0, 6.0, ((0, 4), (1, 4)))
    sinks = jnp.clip(jax.random.uniform(arg_keys[4], (QUERY_HEADS,), jnp.float32, 0.0, 6.0), 0.0, 6.0)
    doc_ids = jax.vmap(lambda own: jnp.searchsorted(jnp.cumsum(ragged(own, SEQS, PACK_TOKENS, DOC_MOST, 1)), jnp.arange(PACK_TOKENS), side="right"))(jax.random.split(own_keys[5], BATCH_PACKS)).reshape((BATCH_PACKS, PACK_TOKENS)).astype(jnp.int32)
    swap_flags = draw_swap_flags(jax.random.fold_in(jax.random.fold_in(arg_keys[7], part), 71), part)
    return {"queries": queries, "keys": keys, "values": values, "grad_out": grad_out, "sinks": sinks, "doc_ids": doc_ids, "swap_flags": swap_flags}


def attend(query_matrix, key_matrix, value_matrix, gradient_rows, sink_scores_raw, query_docs, key_docs, query_pos, key_pos):
    query_count = query_matrix.shape[0]
    key_count = key_matrix.shape[0]
    heads_per_group = QUERY_HEADS // KEY_VALUE_HEADS
    score_scale = 1.0 / math.sqrt(HEAD_SIZE)
    queries_float = query_matrix.astype(jnp.float32).reshape(query_count, KEY_VALUE_HEADS, heads_per_group, HEAD_SIZE)
    gradients_float = gradient_rows.astype(jnp.float32).reshape(query_count, KEY_VALUE_HEADS, heads_per_group, HEAD_SIZE)
    keys_float = key_matrix.astype(jnp.float32).reshape(key_count, KEY_VALUE_HEADS, HEAD_SIZE)
    values_float = value_matrix.astype(jnp.float32).reshape(key_count, KEY_VALUE_HEADS, HEAD_SIZE)
    scores = jnp.einsum('rkgd,lkd->kgrl', queries_float, keys_float) * score_scale
    distance = query_pos[:, None] - key_pos[None, :]
    allowed = (query_docs[:, None] == key_docs[None, :]) & (distance >= 0) & (distance < WINDOW)
    sink_fraction = sink_scores_raw.astype(jnp.float32).reshape(KEY_VALUE_HEADS, heads_per_group)[:, :, None]
    masked = jnp.where(allowed, scores, jnp.float32(-1e+30))
    top = jnp.maximum(lax.optimization_barrier(jnp.max(masked, axis=-1)), sink_fraction)
    expo = jnp.where(allowed, jnp.exp(masked - top[..., None]), jnp.float32(0.0))
    total = jnp.exp(sink_fraction - top) + lax.optimization_barrier(jnp.sum(expo, axis=-1))
    probs = expo / total[..., None]
    probs_b = lax.optimization_barrier(probs.astype(jnp.bfloat16)).astype(jnp.float32)
    out_f = jnp.einsum('kgrl,lkd->rkgd', probs_b, values_float)
    output_blocks = lax.optimization_barrier(out_f.astype(jnp.bfloat16))
    row_dot = jnp.einsum('rkgd,rkgd->kgr', gradients_float, output_blocks.astype(jnp.float32))
    dprobs = jnp.einsum('rkgd,lkd->kgrl', gradients_float, values_float)
    dscores = probs * (dprobs - row_dot[..., None])
    dscores_b = lax.optimization_barrier(dscores.astype(jnp.bfloat16)).astype(jnp.float32)
    query_gradient = (jnp.einsum('kgrl,lkd->rkgd', dscores_b, keys_float) * score_scale).astype(jnp.bfloat16)
    key_gradient = jnp.einsum('kgrl,rkgd->lkd', dscores_b, queries_float) * score_scale
    value_gradient = jnp.einsum('kgrl,rkgd->lkd', probs_b, gradients_float)
    return (output_blocks.reshape(query_count, QUERY_HEADS * HEAD_SIZE), query_gradient.reshape(query_count, QUERY_HEADS * HEAD_SIZE), key_gradient.reshape(key_count, KEY_VALUE_HEADS * HEAD_SIZE), value_gradient.reshape(key_count, KEY_VALUE_HEADS * HEAD_SIZE))

def reference(queries, keys, values, grad_out, sinks, doc_ids, swap_flags):

    def trade_blocks(array):
        width = array.shape[-1]
        shaped = array.reshape(BATCH_PACKS, STRETCHES, BLOCKS, BLK, width)
        partnered = jnp.roll(shaped, BATCH_PACKS // 2, axis=0)
        traded = jnp.where(swap_flags[:, :, :, None, None] == 1, partnered, shaped)
        return traded.reshape(BATCH_PACKS, PACK_TOKENS, width)
    packed_q = trade_blocks(queries)
    packed_k = trade_blocks(keys)
    packed_v = trade_blocks(values)
    packed_g = trade_blocks(grad_out)
    key_span_width = KEY_VALUE_HEADS * HEAD_SIZE
    span = ROWS + WINDOW

    def one_pack(inputs):
        pack_q, pack_k, pack_v, pack_g, pack_docs = inputs
        keys_pad = jnp.concatenate([jnp.zeros((WINDOW, key_span_width), pack_k.dtype), pack_k], axis=0)
        values_pad = jnp.concatenate([jnp.zeros((WINDOW, key_span_width), pack_v.dtype), pack_v], axis=0)
        docs_pad = jnp.concatenate([jnp.full((WINDOW,), -1, jnp.int32), pack_docs.astype(jnp.int32)], axis=0)

        def run_step(running, run_index):
            grad_k_acc, grad_v_acc = running
            offset = (run_index * ROWS).astype(jnp.int32)
            query_matrix = lax.dynamic_slice_in_dim(pack_q, offset, ROWS, 0)
            gradient_rows = lax.dynamic_slice_in_dim(pack_g, offset, ROWS, 0)
            key_matrix = lax.dynamic_slice_in_dim(keys_pad, offset, span, 0)
            value_matrix = lax.dynamic_slice_in_dim(values_pad, offset, span, 0)
            query_docs = lax.dynamic_slice_in_dim(pack_docs.astype(jnp.int32), offset, ROWS, 0)
            key_docs = lax.dynamic_slice_in_dim(docs_pad, offset, span, 0)
            query_pos = offset + jnp.arange(ROWS, dtype=jnp.int32)
            key_pos = offset - WINDOW + jnp.arange(span, dtype=jnp.int32)
            output_blocks, query_gradient, key_gradient, value_gradient = attend(query_matrix, key_matrix, value_matrix, gradient_rows, sinks, query_docs, key_docs, query_pos, key_pos)
            old_k = lax.dynamic_slice_in_dim(grad_k_acc, offset, span, 0)
            old_v = lax.dynamic_slice_in_dim(grad_v_acc, offset, span, 0)
            grad_k_acc = lax.dynamic_update_slice_in_dim(grad_k_acc, old_k + key_gradient, offset, 0)
            grad_v_acc = lax.dynamic_update_slice_in_dim(grad_v_acc, old_v + value_gradient, offset, 0)
            return ((grad_k_acc, grad_v_acc), (output_blocks, query_gradient))
        start_state = (jnp.zeros((PACK_TOKENS + WINDOW, key_span_width), jnp.float32), jnp.zeros((PACK_TOKENS + WINDOW, key_span_width), jnp.float32))
        (grad_k_acc, grad_v_acc), (outs_b, grads_q) = lax.scan(run_step, start_state, jnp.arange(STRETCHES, dtype=jnp.int32))
        return (outs_b.reshape(PACK_TOKENS, QUERY_HEADS * HEAD_SIZE), grads_q.reshape(PACK_TOKENS, QUERY_HEADS * HEAD_SIZE), grad_k_acc[WINDOW:].astype(jnp.bfloat16), grad_v_acc[WINDOW:].astype(jnp.bfloat16))
    packed_out, packed_dq, packed_dk, packed_dv = lax.map(one_pack, (packed_q, packed_k, packed_v, packed_g, doc_ids))
    return (trade_blocks(packed_out), trade_blocks(packed_dq), trade_blocks(packed_dk), trade_blocks(packed_dv))
```

```python
import functools
import math

import jax
import jax.numpy as jnp
from jax import lax
from jax.experimental import pallas as pl
from jax.experimental.pallas import tpu as pltpu
from jax.sharding import PartitionSpec as P

KEY_VALUE_HEADS = 4
HEAD_SIZE = 64
WINDOW = 128
MESH = pl.DeviceIdType.MESH
F32 = jnp.float32
BF16 = jnp.bfloat16
NT = (((1,), (1,)), ((), ()))
NN = (((1,), (0,)), ((), ()))
TN = (((0,), (0,)), ((), ()))


def mm(a, b, dims):
    return lax.dot_general(a, b, dims, preferred_element_type=F32)


def kernel(
    dims,
    flags, sinks, docs, q_hbm, k_hbm, v_hbm, g_hbm,
    out_hbm, dq_hbm, dk_hbm, dv_hbm,
    kv, qv, gv, qp, gp, ov, dqv, dkv, dkv_t,
    kk, vv, bias, mask, hmask, scores, probs, probs_b, ds_b,
    kv_send, kv_in, kv_diag, tail_in, fl_send, fl_in,
    qg_send, qg_in, hg_send, hg_in, og_send, og_in, dkv_send, dkv_in,
    load_sem, qload_sem, gload_sem, store_sem, sem_kv, sem_diag, sem_tail, sem_fl,
    sem_qg, sem_hg, sem_og, sem_dkv,
):
    rows, groups, width, pairs, blocks, blk = dims
    chunks = rows // WINDOW
    kvw = groups * HEAD_SIZE
    dp, ctx = lax.axis_index("dp"), lax.axis_index("ctx")
    dps, ctxs = lax.axis_size("dp"), lax.axis_size("ctx")
    partner = lax.rem(dp + dps // 2, dps)
    right = lax.rem(ctx + 1, ctxs)
    left = lax.rem(ctx + ctxs - 1, ctxs)

    def send(src, dst, sems, where):
        return pltpu.make_async_remote_copy(
            src_ref=src, dst_ref=dst, send_sem=sems.at[0], recv_sem=sems.at[1],
            device_id=where, device_id_type=MESH,
        )

    k_load = pltpu.make_async_copy(k_hbm, kv.at[:, pl.ds(0, kvw)], load_sem.at[0])
    v_load = pltpu.make_async_copy(v_hbm, kv.at[:, pl.ds(kvw, kvw)], load_sem.at[1])
    k_load.start()
    v_load.start()

    def q_load(i):
        return pltpu.make_async_copy(q_hbm.at[:, pl.ds(i * width, width)], qv.at[i], qload_sem.at[i])

    def g_load(i):
        return pltpu.make_async_copy(g_hbm.at[:, pl.ds(i * width, width)], gv.at[i], gload_sem.at[i])

    for i in range(groups):
        q_load(i).start()
        g_load(i).start()

    peers = (
        {"dp": partner}, {"ctx": right}, {"ctx": left},
        {"dp": partner, "ctx": right}, {"dp": partner, "ctx": left},
    )
    barrier = pltpu.get_barrier_semaphore()
    for peer in peers:
        pl.semaphore_signal(barrier, inc=1, device_id=peer, device_id_type=MESH)

    for j in range(blocks):
        value = flags[j].astype(F32)
        mask[j * blk : (j + 1) * blk, :] = jnp.full((blk, 128), value, F32).astype(BF16)

    def picked(ref, lead, lanes):
        block = jnp.zeros((blk, 128), BF16)
        for j in range(blocks):
            at = slice(j * blk, (j + 1) * blk)
            block = jnp.where(mask[at, :] > 0, ref[lead + (at, lanes)], block)
        return block

    tail_blocks = WINDOW // blk
    line = lax.broadcasted_iota(jnp.int32, (tail_blocks, 128), 0)
    tail_flags = jnp.zeros((tail_blocks, 128), F32)
    for j in range(tail_blocks):
        value = flags[blocks - tail_blocks + j].astype(F32)
        tail_flags = jnp.where(line == j, value, tail_flags)
    fl_send[...] = tail_flags

    k_load.wait()
    v_load.wait()
    for a in range(groups):
        lanes = slice(a * 128, (a + 1) * 128)
        kv_send[:, lanes] = picked(kv, (), lanes)
    pl.semaphore_wait(barrier, len(peers))
    kv_copy = send(kv_send, kv_in, sem_kv, {"dp": partner})
    diag_copy = send(kv_send, kv_diag, sem_diag, {"dp": partner, "ctx": right})
    fl_copy = send(fl_send, fl_in, sem_fl, {"ctx": right})
    tail_copy = send(kv.at[pl.ds(rows - WINDOW, WINDOW), :], tail_in, sem_tail, {"ctx": right})
    kv_copy.start()
    diag_copy.start()
    fl_copy.start()
    tail_copy.start()

    def qg_copy(i):
        return send(qg_send.at[i], qg_in.at[i], sem_qg.at[i], {"dp": partner})

    for i in range(groups):
        q_load(i).wait()
        g_load(i).wait()
        for a in range(pairs):
            lanes = slice(a * 128, (a + 1) * 128)
            qg_send[i, :, lanes] = picked(qv, (i,), lanes)
            qg_send[i, :, width + a * 128 : width + (a + 1) * 128] = picked(gv, (i,), lanes)
        qg_copy(i).start()

    offset = ctx * rows
    near = jnp.maximum(offset - WINDOW, 0)
    halo_docs = docs[:, pl.ds(pl.multiple_of(near, 128), WINDOW)]
    halo_docs = jnp.where(ctx == 0, -1, halo_docs)
    own_docs = docs[:, pl.ds(pl.multiple_of(offset, 128), rows)]
    key_docs = jnp.concatenate([halo_docs, own_docs], axis=1).astype(F32)
    dist = (
        lax.broadcasted_iota(jnp.int32, (WINDOW, 2 * WINDOW), 0)
        + WINDOW
        - lax.broadcasted_iota(jnp.int32, (WINDOW, 2 * WINDOW), 1)
    )
    near_enough = (dist >= 0) & (dist < WINDOW)
    for c in range(chunks):
        lanes = jnp.broadcast_to(key_docs[:, (c + 1) * WINDOW : (c + 2) * WINDOW], (WINDOW, WINDOW))
        turned = jnp.transpose(lanes)
        column = jnp.concatenate([turned, turned], axis=1)
        these = jnp.broadcast_to(key_docs[:, c * WINDOW : (c + 2) * WINDOW], (WINDOW, 2 * WINDOW))
        bias[c] = jnp.where((column == these) & near_enough, F32(0.0), F32(-1e30))

    kv_copy.wait_recv()
    diag_copy.wait_recv()
    fl_copy.wait_recv()
    tail_copy.wait_recv()
    hmask[...] = jnp.broadcast_to(fl_in[...][:, None, :], (tail_blocks, blk, 128)).reshape(WINDOW, 128).astype(BF16)

    def merged(mask_ref, first, count, block, own):
        spread = jnp.concatenate([block] * (count // blk), axis=0)
        return jnp.where(mask_ref[first : first + count, :] > 0, spread, own)

    source = lax.broadcasted_iota(jnp.int32, (128, 256), 0)
    target = lax.broadcasted_iota(jnp.int32, (128, 256), 1)
    half = HEAD_SIZE
    scale = 1.0 / math.sqrt(HEAD_SIZE)
    for pair in range(2 * groups // 2):
        at = pair * 128
        halo = merged(hmask, 0, WINDOW, kv_diag[:, at : at + 128], tail_in[:, at : at + 128])
        own = merged(mask, 0, rows, kv_in[:, at : at + 128], kv[:, at : at + 128])
        both = jnp.concatenate([halo, own], axis=0)
        is_key = at < kvw
        for parity in range(2):
            group = (at % kvw) // half + parity
            place = source - parity * half
            valid = (place >= 0) & (place < half)
            pick = valid & ((target == place) | (target == place + 128 + half))
            weight = jnp.where(pick, F32(scale if is_key else 1.0), F32(0.0)).astype(BF16)
            laid = mm(both, weight, NN).astype(BF16)
            ref = kk if is_key else vv
            for c in range(chunks):
                ref[group, c, : 2 * WINDOW, :] = laid[c * WINDOW : (c + 2) * WINDOW, :128]
                ref[group, c, 2 * WINDOW :, :] = laid[c * WINDOW : (c + 2) * WINDOW, 128:]

    def hg_copy(i):
        return send(hg_send.at[i], hg_in.at[i], sem_hg.at[i], {"ctx": left})

    def og_copy(i):
        return send(og_send.at[i], og_in.at[i], sem_og.at[i], {"dp": partner})

    low = lax.broadcasted_iota(jnp.int32, (pairs * WINDOW, 128), 1) < half

    def group_step(i, carry):
        qg_copy(i).wait_recv()
        for c in range(chunks):
            for a in range(pairs):
                lanes = slice(a * 128, (a + 1) * 128)
                mine = slice(c * WINDOW, (c + 1) * WINDOW)
                there = slice(width + a * 128, width + (a + 1) * 128)
                qp[c, a * WINDOW : (a + 1) * WINDOW, :] = merged(
                    mask, c * WINDOW, WINDOW, qg_in[i, :, lanes], qv[i, mine, lanes]
                )
                gp[c, a * WINDOW : (a + 1) * WINDOW, :] = merged(
                    mask, c * WINDOW, WINDOW, qg_in[i, :, there], gv[i, mine, lanes]
                )
        for c in range(chunks):
            q_c, g_c, k_c, v_c = qp[c], gp[c], kk[i, c], vv[i, c]
            scores[...] = mm(q_c, k_c, NT)
            for a in range(pairs):
                for parity in range(2):
                    at_r = slice(a * WINDOW, (a + 1) * WINDOW)
                    at_c = slice(parity * 2 * WINDOW, (parity + 1) * 2 * WINDOW)
                    sink = sinks[i * (2 * pairs) + 2 * a + parity]
                    s = scores[at_r, at_c] + bias[c]
                    top = jnp.maximum(jnp.max(s, axis=1, keepdims=True), sink)
                    e = jnp.exp(s - top)
                    total = jnp.exp(sink - top) + jnp.sum(e, axis=1, keepdims=True)
                    p = e * (1.0 / total)
                    probs[at_r, at_c] = p
                    probs_b[at_r, at_c] = p.astype(BF16)
            p_c = probs_b[...]
            out = mm(p_c, v_c, NN).astype(BF16)
            product = g_c.astype(F32) * out.astype(F32)
            even = jnp.sum(jnp.where(low, product, 0.0), axis=1, keepdims=True)
            odd = jnp.sum(jnp.where(low, 0.0, product), axis=1, keepdims=True)
            scores[...] = mm(g_c, v_c, NT)
            for parity, dot in ((0, even), (1, odd)):
                at_c = slice(parity * 2 * WINDOW, (parity + 1) * 2 * WINDOW)
                ds_b[:, at_c] = (probs[:, at_c] * (scores[:, at_c] - dot)).astype(BF16)
            ds = ds_b[...]
            dq = mm(ds, k_c, NN).astype(BF16)
            mine = slice(c * WINDOW, (c + 1) * WINDOW)
            for a in range(pairs):
                lanes = slice(a * 128, (a + 1) * 128)
                ov[i, mine, lanes] = out[a * WINDOW : (a + 1) * WINDOW]
                dqv[i, mine, lanes] = dq[a * WINDOW : (a + 1) * WINDOW]
            dkt = mm(q_c, ds, TN) * scale
            dvt = mm(g_c, p_c, TN)
            dkt = dkt[:half, : 2 * WINDOW] + dkt[half:, 2 * WINDOW :]
            dvt = dvt[:half, : 2 * WINDOW] + dvt[half:, 2 * WINDOW :]
            if c == 0:
                hg_send[i, :half, :] = dkt[:, :WINDOW]
                hg_send[i, half:, :] = dvt[:, :WINDOW]
                hg_copy(i).start()
            else:
                old = slice((c - 1) * WINDOW, c * WINDOW)
                dkv_t[i, :half, old] = dkv_t[i, :half, old] + dkt[:, :WINDOW]
                dkv_t[i, half:, old] = dkv_t[i, half:, old] + dvt[:, :WINDOW]
            dkv_t[i, :half, mine] = dkt[:, WINDOW:]
            dkv_t[i, half:, mine] = dvt[:, WINDOW:]
        for a in range(pairs):
            lanes = slice(a * 128, (a + 1) * 128)
            og_send[i, :, lanes] = picked(ov, (i,), lanes)
            og_send[i, :, width + a * 128 : width + (a + 1) * 128] = picked(dqv, (i,), lanes)
        og_copy(i).start()
        return carry

    lax.fori_loop(0, groups, group_step, 0)

    for i in range(groups):
        hg_copy(i).wait_recv()
    last = slice(rows - WINDOW, rows)
    for part in range(2):
        for pair in range(groups // 2):
            stack = []
            for i in (2 * pair, 2 * pair + 1):
                at_h = slice(part * half, (part + 1) * half)
                kept = dkv_t[i, at_h, : rows - WINDOW]
                end = dkv_t[i, at_h, last] + hg_in[i, at_h, :]
                stack.append(jnp.concatenate([kept, end], axis=1))
            both = jnp.concatenate(stack, axis=0)
            at = part * kvw + pair * 128
            dkv[:, at : at + 128] = jnp.transpose(both).astype(BF16)
    for a in range(groups):
        lanes = slice(a * 128, (a + 1) * 128)
        dkv_send[:, lanes] = picked(dkv, (), lanes)
    dkv_copy = send(dkv_send, dkv_in, sem_dkv, {"dp": partner})
    dkv_copy.start()

    def out_store(i):
        return pltpu.make_async_copy(ov.at[i], out_hbm.at[:, pl.ds(i * width, width)], qload_sem.at[i])

    def dq_store(i):
        return pltpu.make_async_copy(dqv.at[i], dq_hbm.at[:, pl.ds(i * width, width)], gload_sem.at[i])

    for i in range(groups):
        og_copy(i).wait_recv()
        for a in range(pairs):
            lanes = slice(a * 128, (a + 1) * 128)
            there = slice(width + a * 128, width + (a + 1) * 128)
            ov[i, :, lanes] = merged(mask, 0, rows, og_in[i, :, lanes], ov[i, :, lanes])
            dqv[i, :, lanes] = merged(mask, 0, rows, og_in[i, :, there], dqv[i, :, lanes])
        out_store(i).start()
        dq_store(i).start()

    dkv_copy.wait_recv()
    for pair in range(groups):
        lanes = slice(pair * 128, (pair + 1) * 128)
        dkv[:, lanes] = merged(mask, 0, rows, dkv_in[:, lanes], dkv[:, lanes])
    dk_store = pltpu.make_async_copy(dkv.at[:, pl.ds(0, kvw)], dk_hbm, store_sem.at[0])
    dv_store = pltpu.make_async_copy(dkv.at[:, pl.ds(kvw, kvw)], dv_hbm, store_sem.at[1])
    dk_store.start()
    dv_store.start()

    kv_copy.wait_send()
    diag_copy.wait_send()
    fl_copy.wait_send()
    tail_copy.wait_send()
    dkv_copy.wait_send()
    for i in range(groups):
        qg_copy(i).wait_send()
        hg_copy(i).wait_send()
        og_copy(i).wait_send()
        out_store(i).wait()
        dq_store(i).wait()
    dk_store.wait()
    dv_store.wait()


def shards(queries, keys, values, grad_out, sinks, doc_ids, swap_flags):
    rows = queries.shape[1]
    full = queries.shape[2]
    kvw = keys.shape[2]
    groups = KEY_VALUE_HEADS
    width = full // groups
    pairs = width // 128
    blocks = swap_flags.shape[2]
    blk = rows // blocks
    chunks = rows // WINDOW
    dims = (rows, groups, width, pairs, blocks, blk)
    vm = pltpu.VMEM
    dma = pltpu.SemaphoreType.DMA
    stack = pairs * WINDOW
    span = 4 * WINDOW
    scratch = [
        vm((rows, 2 * kvw), BF16),
        vm((groups, rows, width), BF16), vm((groups, rows, width), BF16),
        vm((chunks, stack, 128), BF16), vm((chunks, stack, 128), BF16),
        vm((groups, rows, width), BF16), vm((groups, rows, width), BF16),
        vm((rows, 2 * kvw), BF16), vm((groups, 2 * HEAD_SIZE, rows), F32),
        vm((groups, chunks, span, 128), BF16), vm((groups, chunks, span, 128), BF16),
        vm((chunks, WINDOW, 2 * WINDOW), F32), vm((rows, 128), BF16), vm((WINDOW, 128), BF16),
        vm((stack, span), F32), vm((stack, span), F32), vm((stack, span), BF16), vm((stack, span), BF16),
        vm((blk, 2 * kvw), BF16), vm((blk, 2 * kvw), BF16), vm((blk, 2 * kvw), BF16),
        vm((WINDOW, 2 * kvw), BF16), vm((WINDOW // blk, 128), F32), vm((WINDOW // blk, 128), F32),
        vm((groups, blk, 2 * width), BF16), vm((groups, blk, 2 * width), BF16),
        vm((groups, 2 * HEAD_SIZE, WINDOW), F32), vm((groups, 2 * HEAD_SIZE, WINDOW), F32),
        vm((groups, blk, 2 * width), BF16), vm((groups, blk, 2 * width), BF16),
        vm((blk, 2 * kvw), BF16), vm((blk, 2 * kvw), BF16),
        dma((2,)), dma((groups,)), dma((groups,)), dma((2,)),
        dma((2,)), dma((2,)), dma((2,)), dma((2,)),
        dma((groups, 2)), dma((groups, 2)), dma((groups, 2)), dma((2,)),
    ]
    hbm = pl.BlockSpec(memory_space=pl.ANY)
    smem = pl.BlockSpec(memory_space=pltpu.SMEM)
    big = jax.ShapeDtypeStruct((rows, full), BF16)
    small = jax.ShapeDtypeStruct((rows, kvw), BF16)
    results = pl.pallas_call(
        functools.partial(kernel, dims),
        out_shape=(big, big, small, small),
        in_specs=[smem, smem, pl.BlockSpec(memory_space=pltpu.VMEM), hbm, hbm, hbm, hbm],
        out_specs=(hbm, hbm, hbm, hbm),
        scratch_shapes=scratch,
        compiler_params=pltpu.CompilerParams(
            collective_id=0, has_side_effects=True, vmem_limit_bytes=48 * 1024 * 1024
        ),
        cost_estimate=pl.CostEstimate(
            flops=10 * rows * full * 2 * WINDOW, bytes_accessed=8 * rows * full, transcendentals=0
        ),
    )(swap_flags[0, 0], sinks, doc_ids, queries[0], keys[0], values[0], grad_out[0])
    return tuple(result[None] for result in results)


def solution(mesh):
    rows_spec = P(("groups", "dp"), "ctx", None)
    in_specs = (rows_spec, rows_spec, rows_spec, rows_spec, P(), P(("groups", "dp"), None), rows_spec)
    return jax.shard_map(
        shards, mesh=mesh, in_specs=in_specs, out_specs=(rows_spec,) * 4, check_vma=False
    )
```

```python
import functools
import math

import jax
import jax.numpy as jnp
from jax import lax
from jax.experimental import pallas as pl
from jax.experimental.pallas import tpu as pltpu
from jax.sharding import PartitionSpec as P

KEY_VALUE_HEADS = 4
HEAD_SIZE = 64
WINDOW = 128
MESH = pl.DeviceIdType.MESH
F32 = jnp.float32
BF16 = jnp.bfloat16
NT = (((1,), (1,)), ((), ()))
NN = (((1,), (0,)), ((), ()))
TN = (((0,), (0,)), ((), ()))


def mm(a, b, dims):
    return lax.dot_general(a, b, dims, preferred_element_type=F32)


def kernel(
    dims,
    flags, sinks, docs, q_hbm, k_hbm, v_hbm, g_hbm,
    out_hbm, dq_hbm, dk_hbm, dv_hbm,
    kv, qv, gv, qp, gp, ov, dqv, dkv, dkv_t,
    kk, vv, bias, mask, hmask, scores, dprobs, probs_b, ds_b,
    kv_send, kv_in, kv_diag, tail_in, fl_send, fl_in,
    qg_send, qg_in, hg_send, hg_in, og_send, og_in, dkv_send, dkv_in,
    load_sem, qload_sem, gload_sem, store_sem, sem_kv, sem_diag, sem_tail, sem_fl,
    sem_qg, sem_hg, sem_og, sem_dkv,
):
    rows, groups, width, pairs, blocks, blk = dims
    chunks = rows // WINDOW
    kvw = groups * HEAD_SIZE
    dp, ctx = lax.axis_index("dp"), lax.axis_index("ctx")
    dps, ctxs = lax.axis_size("dp"), lax.axis_size("ctx")
    partner = lax.rem(dp + dps // 2, dps)
    right = lax.rem(ctx + 1, ctxs)
    left = lax.rem(ctx + ctxs - 1, ctxs)

    def send(src, dst, sems, where):
        return pltpu.make_async_remote_copy(
            src_ref=src, dst_ref=dst, send_sem=sems.at[0], recv_sem=sems.at[1],
            device_id=where, device_id_type=MESH,
        )

    k_load = pltpu.make_async_copy(k_hbm, kv.at[:, pl.ds(0, kvw)], load_sem.at[0])
    v_load = pltpu.make_async_copy(v_hbm, kv.at[:, pl.ds(kvw, kvw)], load_sem.at[1])
    k_load.start()
    v_load.start()

    def q_load(i):
        return pltpu.make_async_copy(q_hbm.at[:, pl.ds(i * width, width)], qv.at[i], qload_sem.at[i])

    def g_load(i):
        return pltpu.make_async_copy(g_hbm.at[:, pl.ds(i * width, width)], gv.at[i], gload_sem.at[i])

    for i in range(groups):
        q_load(i).start()
        g_load(i).start()

    peers = (
        {"dp": partner}, {"ctx": right}, {"ctx": left},
        {"dp": partner, "ctx": right}, {"dp": partner, "ctx": left},
    )
    barrier = pltpu.get_barrier_semaphore()
    for peer in peers:
        pl.semaphore_signal(barrier, inc=1, device_id=peer, device_id_type=MESH)

    for j in range(blocks):
        value = flags[j].astype(F32)
        mask[j * blk : (j + 1) * blk, :] = jnp.full((blk, 128), value, F32).astype(BF16)

    def picked(ref, lead, lanes):
        block = jnp.zeros((blk, 128), BF16)
        for j in range(blocks):
            at = slice(j * blk, (j + 1) * blk)
            block = jnp.where(mask[at, :] > 0, ref[lead + (at, lanes)], block)
        return block

    tail_blocks = WINDOW // blk
    line = lax.broadcasted_iota(jnp.int32, (tail_blocks, 128), 0)
    tail_flags = jnp.zeros((tail_blocks, 128), F32)
    for j in range(tail_blocks):
        value = flags[blocks - tail_blocks + j].astype(F32)
        tail_flags = jnp.where(line == j, value, tail_flags)
    fl_send[...] = tail_flags

    k_load.wait()
    v_load.wait()
    for a in range(groups):
        lanes = slice(a * 128, (a + 1) * 128)
        kv_send[:, lanes] = picked(kv, (), lanes)
    pl.semaphore_wait(barrier, len(peers))
    kv_copy = send(kv_send, kv_in, sem_kv, {"dp": partner})
    diag_copy = send(kv_send, kv_diag, sem_diag, {"dp": partner, "ctx": right})
    fl_copy = send(fl_send, fl_in, sem_fl, {"ctx": right})
    tail_copy = send(kv.at[pl.ds(rows - WINDOW, WINDOW), :], tail_in, sem_tail, {"ctx": right})
    kv_copy.start()
    diag_copy.start()
    fl_copy.start()
    tail_copy.start()

    def qg_copy(i):
        return send(qg_send.at[i], qg_in.at[i], sem_qg.at[i], {"dp": partner})

    for i in range(groups):
        q_load(i).wait()
        g_load(i).wait()
        for a in range(pairs):
            lanes = slice(a * 128, (a + 1) * 128)
            qg_send[i, :, lanes] = picked(qv, (i,), lanes)
            qg_send[i, :, width + a * 128 : width + (a + 1) * 128] = picked(gv, (i,), lanes)
        qg_copy(i).start()

    offset = ctx * rows
    near = jnp.maximum(offset - WINDOW, 0)
    halo_docs = docs[:, pl.ds(pl.multiple_of(near, 128), WINDOW)]
    halo_docs = jnp.where(ctx == 0, -1, halo_docs)
    own_docs = docs[:, pl.ds(pl.multiple_of(offset, 128), rows)]
    key_docs = jnp.concatenate([halo_docs, own_docs], axis=1).astype(F32)
    dist = (
        lax.broadcasted_iota(jnp.int32, (WINDOW, 2 * WINDOW), 0)
        + WINDOW
        - lax.broadcasted_iota(jnp.int32, (WINDOW, 2 * WINDOW), 1)
    )
    near_enough = (dist >= 0) & (dist < WINDOW)
    for c in range(chunks):
        lanes = jnp.broadcast_to(key_docs[:, (c + 1) * WINDOW : (c + 2) * WINDOW], (WINDOW, WINDOW))
        turned = jnp.transpose(lanes)
        column = jnp.concatenate([turned, turned], axis=1)
        these = jnp.broadcast_to(key_docs[:, c * WINDOW : (c + 2) * WINDOW], (WINDOW, 2 * WINDOW))
        bias[c] = jnp.where((column == these) & near_enough, F32(0.0), F32(-1e30))

    kv_copy.wait_recv()
    diag_copy.wait_recv()
    fl_copy.wait_recv()
    tail_copy.wait_recv()
    hmask[...] = jnp.broadcast_to(fl_in[...][:, None, :], (tail_blocks, blk, 128)).reshape(WINDOW, 128).astype(BF16)

    def merged(mask_ref, first, count, block, own):
        spread = jnp.concatenate([block] * (count // blk), axis=0)
        return jnp.where(mask_ref[first : first + count, :] > 0, spread, own)

    source = lax.broadcasted_iota(jnp.int32, (128, 256), 0)
    target = lax.broadcasted_iota(jnp.int32, (128, 256), 1)
    half = HEAD_SIZE
    scale = 1.0 / math.sqrt(HEAD_SIZE)
    for pair in range(2 * groups // 2):
        at = pair * 128
        halo = merged(hmask, 0, WINDOW, kv_diag[:, at : at + 128], tail_in[:, at : at + 128])
        own = merged(mask, 0, rows, kv_in[:, at : at + 128], kv[:, at : at + 128])
        both = jnp.concatenate([halo, own], axis=0)
        is_key = at < kvw
        for parity in range(2):
            group = (at % kvw) // half + parity
            place = source - parity * half
            valid = (place >= 0) & (place < half)
            pick = valid & ((target == place) | (target == place + 128 + half))
            weight = jnp.where(pick, F32(scale if is_key else 1.0), F32(0.0)).astype(BF16)
            laid = mm(both, weight, NN).astype(BF16)
            ref = kk if is_key else vv
            for c in range(chunks):
                ref[group, c, : 2 * WINDOW, :] = laid[c * WINDOW : (c + 2) * WINDOW, :128]
                ref[group, c, 2 * WINDOW :, :] = laid[c * WINDOW : (c + 2) * WINDOW, 128:]

    def hg_copy(i):
        return send(hg_send.at[i], hg_in.at[i], sem_hg.at[i], {"ctx": left})

    def og_copy(i):
        return send(og_send.at[i], og_in.at[i], sem_og.at[i], {"dp": partner})

    low = lax.broadcasted_iota(jnp.int32, (pairs * WINDOW, 128), 1) < half

    def group_step(i, carry):
        qg_copy(i).wait_recv()
        for c in range(chunks):
            for a in range(pairs):
                lanes = slice(a * 128, (a + 1) * 128)
                mine = slice(c * WINDOW, (c + 1) * WINDOW)
                there = slice(width + a * 128, width + (a + 1) * 128)
                qp[c, a * WINDOW : (a + 1) * WINDOW, :] = merged(
                    mask, c * WINDOW, WINDOW, qg_in[i, :, lanes], qv[i, mine, lanes]
                )
                gp[c, a * WINDOW : (a + 1) * WINDOW, :] = merged(
                    mask, c * WINDOW, WINDOW, qg_in[i, :, there], gv[i, mine, lanes]
                )
        def products(c):
            scores[c] = mm(qp[c], kk[i, c], NT)
            dprobs[c] = mm(gp[c], vv[i, c], NT)

        def softmax(c):
            for a in range(pairs):
                for parity in range(2):
                    at_r = slice(a * WINDOW, (a + 1) * WINDOW)
                    at_c = slice(parity * 2 * WINDOW, (parity + 1) * 2 * WINDOW)
                    sink = sinks[i * (2 * pairs) + 2 * a + parity]
                    s = scores[c, at_r, at_c] + bias[c]
                    top = jnp.maximum(jnp.max(s, axis=1, keepdims=True), sink)
                    e = jnp.exp(s - top)
                    total = jnp.exp(sink - top) + jnp.sum(e, axis=1, keepdims=True)
                    probs_b[c, at_r, at_c] = (e * (1.0 / total)).astype(BF16)

        def outputs(c):
            mine = slice(c * WINDOW, (c + 1) * WINDOW)
            out = mm(probs_b[c], vv[i, c], NN).astype(BF16)
            product = gp[c].astype(F32) * out.astype(F32)
            even = jnp.sum(jnp.where(low, product, 0.0), axis=1, keepdims=True)
            odd = jnp.sum(jnp.where(low, 0.0, product), axis=1, keepdims=True)
            for a in range(pairs):
                at_r = slice(a * WINDOW, (a + 1) * WINDOW)
                ov[i, mine, a * 128 : (a + 1) * 128] = out[at_r]
                for parity, dot in ((0, even), (1, odd)):
                    at_c = slice(parity * 2 * WINDOW, (parity + 1) * 2 * WINDOW)
                    p = probs_b[c, at_r, at_c].astype(F32)
                    ds_b[c, at_r, at_c] = (p * (dprobs[c, at_r, at_c] - dot[at_r])).astype(BF16)

        def gradients(c):
            mine = slice(c * WINDOW, (c + 1) * WINDOW)
            ds = ds_b[c]
            dq = mm(ds, kk[i, c], NN).astype(BF16)
            for a in range(pairs):
                dqv[i, mine, a * 128 : (a + 1) * 128] = dq[a * WINDOW : (a + 1) * WINDOW]
            dkt = mm(qp[c], ds, TN) * scale
            dvt = mm(gp[c], probs_b[c], TN)
            dkt = dkt[:half, : 2 * WINDOW] + dkt[half:, 2 * WINDOW :]
            dvt = dvt[:half, : 2 * WINDOW] + dvt[half:, 2 * WINDOW :]
            if c == 0:
                hg_send[i, :half, :] = dkt[:, :WINDOW]
                hg_send[i, half:, :] = dvt[:, :WINDOW]
            else:
                old = slice((c - 1) * WINDOW, c * WINDOW)
                dkv_t[i, :half, old] = dkv_t[i, :half, old] + dkt[:, :WINDOW]
                dkv_t[i, half:, old] = dkv_t[i, half:, old] + dvt[:, :WINDOW]
            dkv_t[i, :half, mine] = dkt[:, WINDOW:]
            dkv_t[i, half:, mine] = dvt[:, WINDOW:]

        for c in range(chunks):
            products(c)
        softmax(0)
        outputs(0)
        for c in range(chunks):
            if c + 1 < chunks:
                softmax(c + 1)
            gradients(c)
            if c + 1 < chunks:
                outputs(c + 1)
            if c == 0:
                hg_copy(i).start()
        for a in range(pairs):
            lanes = slice(a * 128, (a + 1) * 128)
            og_send[i, :, lanes] = picked(ov, (i,), lanes)
            og_send[i, :, width + a * 128 : width + (a + 1) * 128] = picked(dqv, (i,), lanes)
        og_copy(i).start()
        return carry

    lax.fori_loop(0, groups, group_step, 0)

    for i in range(groups):
        hg_copy(i).wait_recv()
    last = slice(rows - WINDOW, rows)
    for part in range(2):
        for pair in range(groups // 2):
            stack = []
            for i in (2 * pair, 2 * pair + 1):
                at_h = slice(part * half, (part + 1) * half)
                kept = dkv_t[i, at_h, : rows - WINDOW]
                end = dkv_t[i, at_h, last] + hg_in[i, at_h, :]
                stack.append(jnp.concatenate([kept, end], axis=1))
            both = jnp.concatenate(stack, axis=0)
            at = part * kvw + pair * 128
            dkv[:, at : at + 128] = jnp.transpose(both).astype(BF16)
    for a in range(groups):
        lanes = slice(a * 128, (a + 1) * 128)
        dkv_send[:, lanes] = picked(dkv, (), lanes)
    dkv_copy = send(dkv_send, dkv_in, sem_dkv, {"dp": partner})
    dkv_copy.start()

    def out_store(i):
        return pltpu.make_async_copy(ov.at[i], out_hbm.at[:, pl.ds(i * width, width)], qload_sem.at[i])

    def dq_store(i):
        return pltpu.make_async_copy(dqv.at[i], dq_hbm.at[:, pl.ds(i * width, width)], gload_sem.at[i])

    for i in range(groups):
        og_copy(i).wait_recv()
        for a in range(pairs):
            lanes = slice(a * 128, (a + 1) * 128)
            there = slice(width + a * 128, width + (a + 1) * 128)
            ov[i, :, lanes] = merged(mask, 0, rows, og_in[i, :, lanes], ov[i, :, lanes])
            dqv[i, :, lanes] = merged(mask, 0, rows, og_in[i, :, there], dqv[i, :, lanes])
        out_store(i).start()
        dq_store(i).start()

    dkv_copy.wait_recv()
    for pair in range(groups):
        lanes = slice(pair * 128, (pair + 1) * 128)
        dkv[:, lanes] = merged(mask, 0, rows, dkv_in[:, lanes], dkv[:, lanes])
    dk_store = pltpu.make_async_copy(dkv.at[:, pl.ds(0, kvw)], dk_hbm, store_sem.at[0])
    dv_store = pltpu.make_async_copy(dkv.at[:, pl.ds(kvw, kvw)], dv_hbm, store_sem.at[1])
    dk_store.start()
    dv_store.start()

    kv_copy.wait_send()
    diag_copy.wait_send()
    fl_copy.wait_send()
    tail_copy.wait_send()
    dkv_copy.wait_send()
    for i in range(groups):
        qg_copy(i).wait_send()
        hg_copy(i).wait_send()
        og_copy(i).wait_send()
        out_store(i).wait()
        dq_store(i).wait()
    dk_store.wait()
    dv_store.wait()


def shards(queries, keys, values, grad_out, sinks, doc_ids, swap_flags):
    rows = queries.shape[1]
    full = queries.shape[2]
    kvw = keys.shape[2]
    groups = KEY_VALUE_HEADS
    width = full // groups
    pairs = width // 128
    blocks = swap_flags.shape[2]
    blk = rows // blocks
    chunks = rows // WINDOW
    dims = (rows, groups, width, pairs, blocks, blk)
    vm = pltpu.VMEM
    dma = pltpu.SemaphoreType.DMA
    stack = pairs * WINDOW
    span = 4 * WINDOW
    scratch = [
        vm((rows, 2 * kvw), BF16),
        vm((groups, rows, width), BF16), vm((groups, rows, width), BF16),
        vm((chunks, stack, 128), BF16), vm((chunks, stack, 128), BF16),
        vm((groups, rows, width), BF16), vm((groups, rows, width), BF16),
        vm((rows, 2 * kvw), BF16), vm((groups, 2 * HEAD_SIZE, rows), F32),
        vm((groups, chunks, span, 128), BF16), vm((groups, chunks, span, 128), BF16),
        vm((chunks, WINDOW, 2 * WINDOW), F32), vm((rows, 128), BF16), vm((WINDOW, 128), BF16),
        vm((chunks, stack, span), F32), vm((chunks, stack, span), F32),
        vm((chunks, stack, span), BF16), vm((chunks, stack, span), BF16),
        vm((blk, 2 * kvw), BF16), vm((blk, 2 * kvw), BF16), vm((blk, 2 * kvw), BF16),
        vm((WINDOW, 2 * kvw), BF16), vm((WINDOW // blk, 128), F32), vm((WINDOW // blk, 128), F32),
        vm((groups, blk, 2 * width), BF16), vm((groups, blk, 2 * width), BF16),
        vm((groups, 2 * HEAD_SIZE, WINDOW), F32), vm((groups, 2 * HEAD_SIZE, WINDOW), F32),
        vm((groups, blk, 2 * width), BF16), vm((groups, blk, 2 * width), BF16),
        vm((blk, 2 * kvw), BF16), vm((blk, 2 * kvw), BF16),
        dma((2,)), dma((groups,)), dma((groups,)), dma((2,)),
        dma((2,)), dma((2,)), dma((2,)), dma((2,)),
        dma((groups, 2)), dma((groups, 2)), dma((groups, 2)), dma((2,)),
    ]
    hbm = pl.BlockSpec(memory_space=pl.ANY)
    smem = pl.BlockSpec(memory_space=pltpu.SMEM)
    big = jax.ShapeDtypeStruct((rows, full), BF16)
    small = jax.ShapeDtypeStruct((rows, kvw), BF16)
    results = pl.pallas_call(
        functools.partial(kernel, dims),
        out_shape=(big, big, small, small),
        in_specs=[smem, smem, pl.BlockSpec(memory_space=pltpu.VMEM), hbm, hbm, hbm, hbm],
        out_specs=(hbm, hbm, hbm, hbm),
        scratch_shapes=scratch,
        compiler_params=pltpu.CompilerParams(
            collective_id=0, has_side_effects=True, vmem_limit_bytes=65400 * 1024
        ),
        cost_estimate=pl.CostEstimate(
            flops=10 * rows * full * 2 * WINDOW, bytes_accessed=8 * rows * full, transcendentals=0
        ),
    )(swap_flags[0, 0], sinks, doc_ids, queries[0], keys[0], values[0], grad_out[0])
    return tuple(result[None] for result in results)


def solution(mesh):
    rows_spec = P(("groups", "dp"), "ctx", None)
    in_specs = (rows_spec, rows_spec, rows_spec, rows_spec, P(), P(("groups", "dp"), None), rows_spec)
    return jax.shard_map(
        shards, mesh=mesh, in_specs=in_specs, out_specs=(rows_spec,) * 4, check_vma=False
    )
```

```python
import functools
import math

import jax
import jax.numpy as jnp
from jax import lax
from jax.experimental import pallas as pl
from jax.experimental.pallas import tpu as pltpu
from jax.sharding import PartitionSpec as P

KEY_VALUE_HEADS = 4
HEAD_SIZE = 64
WINDOW = 128
MESH = pl.DeviceIdType.MESH
F32 = jnp.float32
BF16 = jnp.bfloat16
NT = (((1,), (1,)), ((), ()))
NN = (((1,), (0,)), ((), ()))
TN = (((0,), (0,)), ((), ()))


def mm(a, b, dims):
    return lax.dot_general(a, b, dims, preferred_element_type=F32)


def kernel(
    dims,
    flags, sinks, docs, q_hbm, k_hbm, v_hbm, g_hbm,
    out_hbm, dq_hbm, dk_hbm, dv_hbm,
    kv, qv, gv, qp, gp, ov, dqv, dkv, dkv_t,
    kk, vv, bias, mask, hmask, scores, dprobs, probs_b, ds_b,
    kv_send, kv_in, kv_diag, tail_in, fl_send, fl_in,
    qg_send, qg_in, hg_send, hg_in, og_send, og_in, dkv_send, dkv_in,
    load_sem, qload_sem, gload_sem, store_sem, sem_kv, sem_diag, sem_tail, sem_fl,
    sem_qg, sem_hg, sem_og, sem_dkv,
):
    rows, groups, width, pairs, blocks, blk = dims
    chunks = rows // WINDOW
    kvw = groups * HEAD_SIZE
    dp, ctx = lax.axis_index("dp"), lax.axis_index("ctx")
    dps, ctxs = lax.axis_size("dp"), lax.axis_size("ctx")
    partner = lax.rem(dp + dps // 2, dps)
    right = lax.rem(ctx + 1, ctxs)
    left = lax.rem(ctx + ctxs - 1, ctxs)

    def send(src, dst, sems, where):
        return pltpu.make_async_remote_copy(
            src_ref=src, dst_ref=dst, send_sem=sems.at[0], recv_sem=sems.at[1],
            device_id=where, device_id_type=MESH,
        )

    k_load = pltpu.make_async_copy(k_hbm, kv.at[:, pl.ds(0, kvw)], load_sem.at[0])
    v_load = pltpu.make_async_copy(v_hbm, kv.at[:, pl.ds(kvw, kvw)], load_sem.at[1])
    k_load.start()
    v_load.start()

    def q_load(i):
        return pltpu.make_async_copy(q_hbm.at[:, pl.ds(i * width, width)], qv.at[i], qload_sem.at[i])

    def g_load(i):
        return pltpu.make_async_copy(g_hbm.at[:, pl.ds(i * width, width)], gv.at[i], gload_sem.at[i])

    for i in range(groups):
        q_load(i).start()
        g_load(i).start()

    peers = (
        {"dp": partner}, {"ctx": right}, {"ctx": left},
        {"dp": partner, "ctx": right}, {"dp": partner, "ctx": left},
    )
    barrier = pltpu.get_barrier_semaphore()
    for peer in peers:
        pl.semaphore_signal(barrier, inc=1, device_id=peer, device_id_type=MESH)

    for j in range(blocks):
        value = flags[j].astype(F32)
        mask[j * blk : (j + 1) * blk, :] = jnp.full((blk, 128), value, F32).astype(BF16)

    def picked(ref, lead, lanes):
        block = jnp.zeros((blk, 128), BF16)
        for j in range(blocks):
            at = slice(j * blk, (j + 1) * blk)
            block = jnp.where(mask[at, :] > 0, ref[lead + (at, lanes)], block)
        return block

    tail_blocks = WINDOW // blk
    line = lax.broadcasted_iota(jnp.int32, (tail_blocks, 128), 0)
    tail_flags = jnp.zeros((tail_blocks, 128), F32)
    for j in range(tail_blocks):
        value = flags[blocks - tail_blocks + j].astype(F32)
        tail_flags = jnp.where(line == j, value, tail_flags)
    fl_send[...] = tail_flags

    k_load.wait()
    v_load.wait()
    for a in range(groups):
        lanes = slice(a * 128, (a + 1) * 128)
        kv_send[:, lanes] = picked(kv, (), lanes)
    pl.semaphore_wait(barrier, len(peers))
    kv_copy = send(kv_send, kv_in, sem_kv, {"dp": partner})
    diag_copy = send(kv_send, kv_diag, sem_diag, {"dp": partner, "ctx": right})
    fl_copy = send(fl_send, fl_in, sem_fl, {"ctx": right})
    tail_copy = send(kv.at[pl.ds(rows - WINDOW, WINDOW), :], tail_in, sem_tail, {"ctx": right})
    kv_copy.start()
    diag_copy.start()
    fl_copy.start()
    tail_copy.start()

    def qg_copy(i):
        return send(qg_send.at[i], qg_in.at[i], sem_qg.at[i], {"dp": partner})

    for i in range(groups):
        q_load(i).wait()
        g_load(i).wait()
        for a in range(pairs):
            lanes = slice(a * 128, (a + 1) * 128)
            qg_send[i, :, lanes] = picked(qv, (i,), lanes)
            qg_send[i, :, width + a * 128 : width + (a + 1) * 128] = picked(gv, (i,), lanes)
        qg_copy(i).start()

    offset = ctx * rows
    near = jnp.maximum(offset - WINDOW, 0)
    halo_docs = docs[:, pl.ds(pl.multiple_of(near, 128), WINDOW)]
    halo_docs = jnp.where(ctx == 0, -1, halo_docs)
    own_docs = docs[:, pl.ds(pl.multiple_of(offset, 128), rows)]
    key_docs = jnp.concatenate([halo_docs, own_docs], axis=1).astype(F32)
    dist = (
        lax.broadcasted_iota(jnp.int32, (WINDOW, 2 * WINDOW), 0)
        + WINDOW
        - lax.broadcasted_iota(jnp.int32, (WINDOW, 2 * WINDOW), 1)
    )
    near_enough = (dist >= 0) & (dist < WINDOW)
    for c in range(chunks):
        lanes = jnp.broadcast_to(key_docs[:, (c + 1) * WINDOW : (c + 2) * WINDOW], (WINDOW, WINDOW))
        turned = jnp.transpose(lanes)
        column = jnp.concatenate([turned, turned], axis=1)
        these = jnp.broadcast_to(key_docs[:, c * WINDOW : (c + 2) * WINDOW], (WINDOW, 2 * WINDOW))
        bias[c] = jnp.where((column == these) & near_enough, F32(0.0), F32(-1e30))

    kv_copy.wait_recv()
    diag_copy.wait_recv()
    fl_copy.wait_recv()
    tail_copy.wait_recv()
    hmask[...] = jnp.broadcast_to(fl_in[...][:, None, :], (tail_blocks, blk, 128)).reshape(WINDOW, 128).astype(BF16)

    def merged(mask_ref, first, count, block, own):
        spread = jnp.concatenate([block] * (count // blk), axis=0)
        return jnp.where(mask_ref[first : first + count, :] > 0, spread, own)

    source = lax.broadcasted_iota(jnp.int32, (128, 256), 0)
    target = lax.broadcasted_iota(jnp.int32, (128, 256), 1)
    half = HEAD_SIZE
    scale = 1.0 / math.sqrt(HEAD_SIZE)
    for pair in range(2 * groups // 2):
        at = pair * 128
        halo = merged(hmask, 0, WINDOW, kv_diag[:, at : at + 128], tail_in[:, at : at + 128])
        own = merged(mask, 0, rows, kv_in[:, at : at + 128], kv[:, at : at + 128])
        both = jnp.concatenate([halo, own], axis=0)
        is_key = at < kvw
        for parity in range(2):
            group = (at % kvw) // half + parity
            place = source - parity * half
            valid = (place >= 0) & (place < half)
            pick = valid & ((target == place) | (target == place + 128 + half))
            weight = jnp.where(pick, F32(scale if is_key else 1.0), F32(0.0)).astype(BF16)
            laid = mm(both, weight, NN).astype(BF16)
            ref = kk if is_key else vv
            for c in range(chunks):
                ref[group, c, : 2 * WINDOW, :] = laid[c * WINDOW : (c + 2) * WINDOW, :128]
                ref[group, c, 2 * WINDOW :, :] = laid[c * WINDOW : (c + 2) * WINDOW, 128:]

    def hg_copy(i):
        return send(hg_send.at[i], hg_in.at[i], sem_hg.at[i], {"ctx": left})

    def og_copy(i):
        return send(og_send.at[i], og_in.at[i], sem_og.at[i], {"dp": partner})

    low = lax.broadcasted_iota(jnp.int32, (pairs * WINDOW, 128), 1) < half

    def group_step(i, carry):
        qg_copy(i).wait_recv()
        for c in range(chunks):
            for a in range(pairs):
                lanes = slice(a * 128, (a + 1) * 128)
                mine = slice(c * WINDOW, (c + 1) * WINDOW)
                there = slice(width + a * 128, width + (a + 1) * 128)
                qp[c, a * WINDOW : (a + 1) * WINDOW, :] = merged(
                    mask, c * WINDOW, WINDOW, qg_in[i, :, lanes], qv[i, mine, lanes]
                )
                gp[c, a * WINDOW : (a + 1) * WINDOW, :] = merged(
                    mask, c * WINDOW, WINDOW, qg_in[i, :, there], gv[i, mine, lanes]
                )
        def products(c):
            scores[c] = mm(qp[c], kk[i, c], NT)
            dprobs[c] = mm(gp[c], vv[i, c], NT)

        def softmax(c):
            for a in range(pairs):
                for parity in range(2):
                    at_r = slice(a * WINDOW, (a + 1) * WINDOW)
                    at_c = slice(parity * 2 * WINDOW, (parity + 1) * 2 * WINDOW)
                    sink = sinks[i * (2 * pairs) + 2 * a + parity]
                    s = scores[c, at_r, at_c] + bias[c]
                    top = jnp.maximum(jnp.max(s, axis=1, keepdims=True), sink)
                    e = jnp.exp(s - top)
                    total = jnp.exp(sink - top) + jnp.sum(e, axis=1, keepdims=True)
                    probs_b[c, at_r, at_c] = (e * (1.0 / total)).astype(BF16)

        def outputs(c):
            mine = slice(c * WINDOW, (c + 1) * WINDOW)
            out = mm(probs_b[c], vv[i, c], NN).astype(BF16)
            product = gp[c].astype(F32) * out.astype(F32)
            even = jnp.sum(jnp.where(low, product, 0.0), axis=1, keepdims=True)
            odd = jnp.sum(jnp.where(low, 0.0, product), axis=1, keepdims=True)
            for a in range(pairs):
                at_r = slice(a * WINDOW, (a + 1) * WINDOW)
                ov[i, mine, a * 128 : (a + 1) * 128] = out[at_r]
                for parity, dot in ((0, even), (1, odd)):
                    at_c = slice(parity * 2 * WINDOW, (parity + 1) * 2 * WINDOW)
                    p = probs_b[c, at_r, at_c].astype(F32)
                    ds_b[c, at_r, at_c] = (p * (dprobs[c, at_r, at_c] - dot[at_r])).astype(BF16)

        def gradients(c):
            mine = slice(c * WINDOW, (c + 1) * WINDOW)
            ds = ds_b[c]
            dq = mm(ds, kk[i, c], NN).astype(BF16)
            for a in range(pairs):
                dqv[i, mine, a * 128 : (a + 1) * 128] = dq[a * WINDOW : (a + 1) * WINDOW]
            dkt = mm(qp[c], ds, TN) * scale
            dvt = mm(gp[c], probs_b[c], TN)
            dkt = dkt[:half, : 2 * WINDOW] + dkt[half:, 2 * WINDOW :]
            dvt = dvt[:half, : 2 * WINDOW] + dvt[half:, 2 * WINDOW :]
            if c == 0:
                hg_send[i, :half, :] = dkt[:, :WINDOW]
                hg_send[i, half:, :] = dvt[:, :WINDOW]
            else:
                old = slice((c - 1) * WINDOW, c * WINDOW)
                dkv_t[i, :half, old] = dkv_t[i, :half, old] + dkt[:, :WINDOW]
                dkv_t[i, half:, old] = dkv_t[i, half:, old] + dvt[:, :WINDOW]
            dkv_t[i, :half, mine] = dkt[:, WINDOW:]
            dkv_t[i, half:, mine] = dvt[:, WINDOW:]

        for c in range(chunks):
            products(c)
        softmax(0)
        outputs(0)
        for c in range(chunks):
            if c + 1 < chunks:
                softmax(c + 1)
            gradients(c)
            if c + 1 < chunks:
                outputs(c + 1)
            if c == 0:
                hg_copy(i).start()
        for a in range(pairs):
            lanes = slice(a * 128, (a + 1) * 128)
            og_send[i, :, lanes] = picked(ov, (i,), lanes)
            og_send[i, :, width + a * 128 : width + (a + 1) * 128] = picked(dqv, (i,), lanes)
        og_copy(i).start()
        return carry

    lax.fori_loop(0, groups, group_step, 0)

    for i in range(groups):
        hg_copy(i).wait_recv()
    last = slice(rows - WINDOW, rows)
    for part in range(2):
        for pair in range(groups // 2):
            stack = []
            for i in (2 * pair, 2 * pair + 1):
                at_h = slice(part * half, (part + 1) * half)
                kept = dkv_t[i, at_h, : rows - WINDOW]
                end = dkv_t[i, at_h, last] + hg_in[i, at_h, :]
                stack.append(jnp.concatenate([kept, end], axis=1))
            both = jnp.concatenate(stack, axis=0)
            at = part * kvw + pair * 128
            dkv[:, at : at + 128] = jnp.transpose(both).astype(BF16)
    for a in range(groups):
        lanes = slice(a * 128, (a + 1) * 128)
        dkv_send[:, lanes] = picked(dkv, (), lanes)
    dkv_copy = send(dkv_send, dkv_in, sem_dkv, {"dp": partner})
    dkv_copy.start()

    def out_store(i):
        return pltpu.make_async_copy(ov.at[i], out_hbm.at[:, pl.ds(i * width, width)], qload_sem.at[i])

    def dq_store(i):
        return pltpu.make_async_copy(dqv.at[i], dq_hbm.at[:, pl.ds(i * width, width)], gload_sem.at[i])

    for i in range(groups):
        og_copy(i).wait_recv()
        for a in range(pairs):
            lanes = slice(a * 128, (a + 1) * 128)
            there = slice(width + a * 128, width + (a + 1) * 128)
            ov[i, :, lanes] = merged(mask, 0, rows, og_in[i, :, lanes], ov[i, :, lanes])
            dqv[i, :, lanes] = merged(mask, 0, rows, og_in[i, :, there], dqv[i, :, lanes])
        out_store(i).start()
        dq_store(i).start()

    dkv_copy.wait_recv()
    for pair in range(groups):
        lanes = slice(pair * 128, (pair + 1) * 128)
        dkv[:, lanes] = merged(mask, 0, rows, dkv_in[:, lanes], dkv[:, lanes])
    dk_store = pltpu.make_async_copy(dkv.at[:, pl.ds(0, kvw)], dk_hbm, store_sem.at[0])
    dv_store = pltpu.make_async_copy(dkv.at[:, pl.ds(kvw, kvw)], dv_hbm, store_sem.at[1])
    dk_store.start()
    dv_store.start()

    kv_copy.wait_send()
    diag_copy.wait_send()
    fl_copy.wait_send()
    tail_copy.wait_send()
    dkv_copy.wait_send()
    for i in range(groups):
        qg_copy(i).wait_send()
        hg_copy(i).wait_send()
        og_copy(i).wait_send()
        out_store(i).wait()
        dq_store(i).wait()
    dk_store.wait()
    dv_store.wait()


def hand_over(parts, *refs):
    count = len(parts)
    sources, targets, held = refs[:count], refs[count : 2 * count], refs[2 * count : 3 * count]
    load_sem, store_sem = refs[3 * count :]
    loads, stores = [], []
    slot = 0
    for n, cuts in enumerate(parts):
        size = sources[n].shape[0] // cuts
        for cut in range(cuts):
            at = pl.ds(cut * size, size)
            loads.append(pltpu.make_async_copy(sources[n].at[at, :], held[n].at[at, :], load_sem.at[slot]))
            stores.append(pltpu.make_async_copy(held[n].at[at, :], targets[n].at[at, :], store_sem.at[slot]))
            slot += 1
    for load in loads:
        load.start()
    for load, store in zip(loads, stores):
        load.wait()
        store.start()
    for store in stores:
        store.wait()


def shards(queries, keys, values, grad_out, sinks, doc_ids, swap_flags):
    rows = queries.shape[1]
    full = queries.shape[2]
    kvw = keys.shape[2]
    groups = KEY_VALUE_HEADS
    width = full // groups
    pairs = width // 128
    blocks = swap_flags.shape[2]
    blk = rows // blocks
    chunks = rows // WINDOW
    dims = (rows, groups, width, pairs, blocks, blk)
    vm = pltpu.VMEM
    dma = pltpu.SemaphoreType.DMA
    stack = pairs * WINDOW
    span = 4 * WINDOW
    scratch = [
        vm((rows, 2 * kvw), BF16),
        vm((groups, rows, width), BF16), vm((groups, rows, width), BF16),
        vm((chunks, stack, 128), BF16), vm((chunks, stack, 128), BF16),
        vm((groups, rows, width), BF16), vm((groups, rows, width), BF16),
        vm((rows, 2 * kvw), BF16), vm((groups, 2 * HEAD_SIZE, rows), F32),
        vm((groups, chunks, span, 128), BF16), vm((groups, chunks, span, 128), BF16),
        vm((chunks, WINDOW, 2 * WINDOW), F32), vm((rows, 128), BF16), vm((WINDOW, 128), BF16),
        vm((chunks, stack, span), F32), vm((chunks, stack, span), F32),
        vm((chunks, stack, span), BF16), vm((chunks, stack, span), BF16),
        vm((blk, 2 * kvw), BF16), vm((blk, 2 * kvw), BF16), vm((blk, 2 * kvw), BF16),
        vm((WINDOW, 2 * kvw), BF16), vm((WINDOW // blk, 128), F32), vm((WINDOW // blk, 128), F32),
        vm((groups, blk, 2 * width), BF16), vm((groups, blk, 2 * width), BF16),
        vm((groups, 2 * HEAD_SIZE, WINDOW), F32), vm((groups, 2 * HEAD_SIZE, WINDOW), F32),
        vm((groups, blk, 2 * width), BF16), vm((groups, blk, 2 * width), BF16),
        vm((blk, 2 * kvw), BF16), vm((blk, 2 * kvw), BF16),
        dma((2,)), dma((groups,)), dma((groups,)), dma((2,)),
        dma((2,)), dma((2,)), dma((2,)), dma((2,)),
        dma((groups, 2)), dma((groups, 2)), dma((groups, 2)), dma((2,)),
    ]
    hbm = pl.BlockSpec(memory_space=pl.ANY)
    smem = pl.BlockSpec(memory_space=pltpu.SMEM)
    big = jax.ShapeDtypeStruct((rows, full), BF16)
    small = jax.ShapeDtypeStruct((rows, kvw), BF16)
    results = pl.pallas_call(
        functools.partial(kernel, dims),
        out_shape=(big, big, small, small),
        in_specs=[smem, smem, pl.BlockSpec(memory_space=pltpu.VMEM), hbm, hbm, hbm, hbm],
        out_specs=(hbm, hbm, hbm, hbm),
        scratch_shapes=scratch,
        compiler_params=pltpu.CompilerParams(
            collective_id=0, has_side_effects=True, vmem_limit_bytes=65400 * 1024
        ),
        cost_estimate=pl.CostEstimate(
            flops=10 * rows * full * 2 * WINDOW, bytes_accessed=8 * rows * full, transcendentals=0
        ),
    )(swap_flags[0, 0], sinks, doc_ids, queries[0], keys[0], values[0], grad_out[0])
    parts = (4, 4, 1, 1)
    shapes = (big, big, small, small)
    results = pl.pallas_call(
        functools.partial(hand_over, parts),
        out_shape=shapes,
        in_specs=[hbm] * len(parts),
        out_specs=(hbm,) * len(parts),
        scratch_shapes=[vm(shape.shape, BF16) for shape in shapes] + [dma((sum(parts),)), dma((sum(parts),))],
        compiler_params=pltpu.CompilerParams(vmem_limit_bytes=65400 * 1024),
        cost_estimate=pl.CostEstimate(flops=0, bytes_accessed=9 * rows * full, transcendentals=0),
    )(*results)
    return tuple(result[None] for result in results)


def solution(mesh):
    rows_spec = P(("groups", "dp"), "ctx", None)
    in_specs = (rows_spec, rows_spec, rows_spec, rows_spec, P(), P(("groups", "dp"), None), rows_spec)
    return jax.shard_map(
        shards, mesh=mesh, in_specs=in_specs, out_specs=(rows_spec,) * 4, check_vma=False
    )
```

```python
import functools
import math

import jax
import jax.numpy as jnp
from jax import lax
from jax.experimental import pallas as pl
from jax.experimental.pallas import tpu as pltpu
from jax.sharding import PartitionSpec as P

KEY_VALUE_HEADS = 4
HEAD_SIZE = 64
WINDOW = 128
MESH = pl.DeviceIdType.MESH
F32 = jnp.float32
BF16 = jnp.bfloat16
NT = (((1,), (1,)), ((), ()))
NN = (((1,), (0,)), ((), ()))
TN = (((0,), (0,)), ((), ()))


def mm(a, b, dims):
    return lax.dot_general(a, b, dims, preferred_element_type=F32)


def kernel(
    dims,
    flags, sinks, docs, q_hbm, k_hbm, v_hbm, g_hbm,
    out_hbm, dq_hbm, dk_hbm, dv_hbm,
    kv, qv, gv, qp, gp, ov, dqv, dkv, dkv_t,
    kk, vv, bias, mask, hmask, scores, dprobs, probs_b, ds_b,
    kv_send, kv_in, kv_diag, tail_in, fl_send, fl_in,
    qg_send, qg_in, hg_send, hg_in, og_send, og_in, dkv_send, dkv_in,
    load_sem, qload_sem, gload_sem, store_sem, sem_kv, sem_diag, sem_tail, sem_fl,
    sem_qg, sem_hg, sem_og, sem_dkv,
):
    rows, groups, width, pairs, blocks, blk = dims
    chunks = rows // WINDOW
    kvw = groups * HEAD_SIZE
    dp, ctx = lax.axis_index("dp"), lax.axis_index("ctx")
    dps, ctxs = lax.axis_size("dp"), lax.axis_size("ctx")
    partner = lax.rem(dp + dps // 2, dps)
    right = lax.rem(ctx + 1, ctxs)
    left = lax.rem(ctx + ctxs - 1, ctxs)

    def send(src, dst, sems, where):
        return pltpu.make_async_remote_copy(
            src_ref=src, dst_ref=dst, send_sem=sems.at[0], recv_sem=sems.at[1],
            device_id=where, device_id_type=MESH,
        )

    k_load = pltpu.make_async_copy(k_hbm, kv.at[:, pl.ds(0, kvw)], load_sem.at[0])
    v_load = pltpu.make_async_copy(v_hbm, kv.at[:, pl.ds(kvw, kvw)], load_sem.at[1])
    k_load.start()
    v_load.start()

    def q_load(i):
        return pltpu.make_async_copy(q_hbm.at[:, pl.ds(i * width, width)], qv.at[i], qload_sem.at[i])

    def g_load(i):
        return pltpu.make_async_copy(g_hbm.at[:, pl.ds(i * width, width)], gv.at[i], gload_sem.at[i])

    for i in range(groups):
        q_load(i).start()
        g_load(i).start()

    peers = (
        {"dp": partner}, {"ctx": right}, {"ctx": left},
        {"dp": partner, "ctx": right}, {"dp": partner, "ctx": left},
    )
    barrier = pltpu.get_barrier_semaphore()
    for peer in peers:
        pl.semaphore_signal(barrier, inc=1, device_id=peer, device_id_type=MESH)

    for j in range(blocks):
        value = flags[j].astype(F32)
        mask[j * blk : (j + 1) * blk, :] = jnp.full((blk, 128), value, F32).astype(BF16)

    def picked(ref, lead, lanes):
        block = jnp.zeros((blk, 128), BF16)
        for j in range(blocks):
            at = slice(j * blk, (j + 1) * blk)
            block = jnp.where(mask[at, :] > 0, ref[lead + (at, lanes)], block)
        return block

    tail_blocks = WINDOW // blk
    line = lax.broadcasted_iota(jnp.int32, (tail_blocks, 128), 0)
    tail_flags = jnp.zeros((tail_blocks, 128), F32)
    for j in range(tail_blocks):
        value = flags[blocks - tail_blocks + j].astype(F32)
        tail_flags = jnp.where(line == j, value, tail_flags)
    fl_send[...] = tail_flags

    k_load.wait()
    v_load.wait()
    for a in range(groups):
        lanes = slice(a * 128, (a + 1) * 128)
        kv_send[:, lanes] = picked(kv, (), lanes)
    pl.semaphore_wait(barrier, len(peers))
    kv_copy = send(kv_send, kv_in, sem_kv, {"dp": partner})
    diag_copy = send(kv_send, kv_diag, sem_diag, {"dp": partner, "ctx": right})
    fl_copy = send(fl_send, fl_in, sem_fl, {"ctx": right})
    tail_copy = send(kv.at[pl.ds(rows - WINDOW, WINDOW), :], tail_in, sem_tail, {"ctx": right})
    kv_copy.start()
    diag_copy.start()
    fl_copy.start()
    tail_copy.start()

    def qg_copy(i):
        return send(qg_send.at[i], qg_in.at[i], sem_qg.at[i], {"dp": partner})

    for i in range(groups):
        q_load(i).wait()
        g_load(i).wait()
        for a in range(pairs):
            lanes = slice(a * 128, (a + 1) * 128)
            qg_send[i, :, lanes] = picked(qv, (i,), lanes)
            qg_send[i, :, width + a * 128 : width + (a + 1) * 128] = picked(gv, (i,), lanes)
        qg_copy(i).start()

    offset = ctx * rows
    near = jnp.maximum(offset - WINDOW, 0)
    halo_docs = docs[:, pl.ds(pl.multiple_of(near, 128), WINDOW)]
    halo_docs = jnp.where(ctx == 0, -1, halo_docs)
    own_docs = docs[:, pl.ds(pl.multiple_of(offset, 128), rows)]
    key_docs = jnp.concatenate([halo_docs, own_docs], axis=1).astype(F32)
    dist = (
        lax.broadcasted_iota(jnp.int32, (WINDOW, 2 * WINDOW), 0)
        + WINDOW
        - lax.broadcasted_iota(jnp.int32, (WINDOW, 2 * WINDOW), 1)
    )
    near_enough = (dist >= 0) & (dist < WINDOW)
    for c in range(chunks):
        lanes = jnp.broadcast_to(key_docs[:, (c + 1) * WINDOW : (c + 2) * WINDOW], (WINDOW, WINDOW))
        turned = jnp.transpose(lanes)
        column = jnp.concatenate([turned, turned], axis=1)
        these = jnp.broadcast_to(key_docs[:, c * WINDOW : (c + 2) * WINDOW], (WINDOW, 2 * WINDOW))
        bias[c] = jnp.where((column == these) & near_enough, F32(0.0), F32(-1e30))

    kv_copy.wait_recv()
    diag_copy.wait_recv()
    fl_copy.wait_recv()
    tail_copy.wait_recv()
    hmask[...] = jnp.broadcast_to(fl_in[...][:, None, :], (tail_blocks, blk, 128)).reshape(WINDOW, 128).astype(BF16)

    def merged(mask_ref, first, count, block, own):
        spread = jnp.concatenate([block] * (count // blk), axis=0)
        return jnp.where(mask_ref[first : first + count, :] > 0, spread, own)

    source = lax.broadcasted_iota(jnp.int32, (128, 256), 0)
    target = lax.broadcasted_iota(jnp.int32, (128, 256), 1)
    half = HEAD_SIZE
    scale = 1.0 / math.sqrt(HEAD_SIZE)
    for pair in range(2 * groups // 2):
        at = pair * 128
        halo = merged(hmask, 0, WINDOW, kv_diag[:, at : at + 128], tail_in[:, at : at + 128])
        own = merged(mask, 0, rows, kv_in[:, at : at + 128], kv[:, at : at + 128])
        both = jnp.concatenate([halo, own], axis=0)
        is_key = at < kvw
        for parity in range(2):
            group = (at % kvw) // half + parity
            place = source - parity * half
            valid = (place >= 0) & (place < half)
            pick = valid & ((target == place) | (target == place + 128 + half))
            weight = jnp.where(pick, F32(scale if is_key else 1.0), F32(0.0)).astype(BF16)
            laid = mm(both, weight, NN).astype(BF16)
            ref = kk if is_key else vv
            for c in range(chunks):
                ref[group, c, : 2 * WINDOW, :] = laid[c * WINDOW : (c + 2) * WINDOW, :128]
                ref[group, c, 2 * WINDOW :, :] = laid[c * WINDOW : (c + 2) * WINDOW, 128:]

    def hg_copy(i):
        return send(hg_send.at[i], hg_in.at[i], sem_hg.at[i], {"ctx": left})

    def og_copy(i):
        return send(og_send.at[i], og_in.at[i], sem_og.at[i], {"dp": partner})

    low = lax.broadcasted_iota(jnp.int32, (pairs * WINDOW, 128), 1) < half

    def group_step(i, carry):
        qg_copy(i).wait_recv()
        for c in range(chunks):
            for a in range(pairs):
                lanes = slice(a * 128, (a + 1) * 128)
                mine = slice(c * WINDOW, (c + 1) * WINDOW)
                there = slice(width + a * 128, width + (a + 1) * 128)
                qp[c, a * WINDOW : (a + 1) * WINDOW, :] = merged(
                    mask, c * WINDOW, WINDOW, qg_in[i, :, lanes], qv[i, mine, lanes]
                )
                gp[c, a * WINDOW : (a + 1) * WINDOW, :] = merged(
                    mask, c * WINDOW, WINDOW, qg_in[i, :, there], gv[i, mine, lanes]
                )
        def products(c):
            scores[c] = mm(qp[c], kk[i, c], NT)
            dprobs[c] = mm(gp[c], vv[i, c], NT)

        def softmax(c):
            for a in range(pairs):
                for parity in range(2):
                    at_r = slice(a * WINDOW, (a + 1) * WINDOW)
                    at_c = slice(parity * 2 * WINDOW, (parity + 1) * 2 * WINDOW)
                    sink = sinks[i * (2 * pairs) + 2 * a + parity]
                    s = scores[c, at_r, at_c] + bias[c]
                    top = jnp.maximum(jnp.max(s, axis=1, keepdims=True), sink)
                    e = jnp.exp(s - top)
                    total = jnp.exp(sink - top) + jnp.sum(e, axis=1, keepdims=True)
                    probs_b[c, at_r, at_c] = (e * (1.0 / total)).astype(BF16)

        def outputs(c):
            mine = slice(c * WINDOW, (c + 1) * WINDOW)
            out = mm(probs_b[c], vv[i, c], NN).astype(BF16)
            product = gp[c].astype(F32) * out.astype(F32)
            even = jnp.sum(jnp.where(low, product, 0.0), axis=1, keepdims=True)
            odd = jnp.sum(jnp.where(low, 0.0, product), axis=1, keepdims=True)
            for a in range(pairs):
                at_r = slice(a * WINDOW, (a + 1) * WINDOW)
                ov[i, mine, a * 128 : (a + 1) * 128] = out[at_r]
                for parity, dot in ((0, even), (1, odd)):
                    at_c = slice(parity * 2 * WINDOW, (parity + 1) * 2 * WINDOW)
                    p = probs_b[c, at_r, at_c].astype(F32)
                    ds_b[c, at_r, at_c] = (p * (dprobs[c, at_r, at_c] - dot[at_r])).astype(BF16)

        def gradients(c):
            mine = slice(c * WINDOW, (c + 1) * WINDOW)
            ds = ds_b[c]
            dq = mm(ds, kk[i, c], NN).astype(BF16)
            for a in range(pairs):
                dqv[i, mine, a * 128 : (a + 1) * 128] = dq[a * WINDOW : (a + 1) * WINDOW]
            dkt = mm(qp[c], ds, TN) * scale
            dvt = mm(gp[c], probs_b[c], TN)
            dkt = dkt[:half, : 2 * WINDOW] + dkt[half:, 2 * WINDOW :]
            dvt = dvt[:half, : 2 * WINDOW] + dvt[half:, 2 * WINDOW :]
            if c == 0:
                hg_send[i, :half, :] = dkt[:, :WINDOW]
                hg_send[i, half:, :] = dvt[:, :WINDOW]
            else:
                old = slice((c - 1) * WINDOW, c * WINDOW)
                dkv_t[i, :half, old] = dkv_t[i, :half, old] + dkt[:, :WINDOW]
                dkv_t[i, half:, old] = dkv_t[i, half:, old] + dvt[:, :WINDOW]
            dkv_t[i, :half, mine] = dkt[:, WINDOW:]
            dkv_t[i, half:, mine] = dvt[:, WINDOW:]

        for c in range(chunks):
            products(c)
        softmax(0)
        outputs(0)
        for c in range(chunks):
            if c + 1 < chunks:
                softmax(c + 1)
            gradients(c)
            if c + 1 < chunks:
                outputs(c + 1)
            if c == 0:
                hg_copy(i).start()
        for a in range(pairs):
            lanes = slice(a * 128, (a + 1) * 128)
            og_send[i, :, lanes] = picked(ov, (i,), lanes)
            og_send[i, :, width + a * 128 : width + (a + 1) * 128] = picked(dqv, (i,), lanes)
        og_copy(i).start()
        return carry

    lax.fori_loop(0, groups, group_step, 0, unroll=2)

    for i in range(groups):
        hg_copy(i).wait_recv()
    last = slice(rows - WINDOW, rows)
    for part in range(2):
        for pair in range(groups // 2):
            stack = []
            for i in (2 * pair, 2 * pair + 1):
                at_h = slice(part * half, (part + 1) * half)
                kept = dkv_t[i, at_h, : rows - WINDOW]
                end = dkv_t[i, at_h, last] + hg_in[i, at_h, :]
                stack.append(jnp.concatenate([kept, end], axis=1))
            both = jnp.concatenate(stack, axis=0)
            at = part * kvw + pair * 128
            dkv[:, at : at + 128] = jnp.transpose(both).astype(BF16)
    for a in range(groups):
        lanes = slice(a * 128, (a + 1) * 128)
        dkv_send[:, lanes] = picked(dkv, (), lanes)
    dkv_copy = send(dkv_send, dkv_in, sem_dkv, {"dp": partner})
    dkv_copy.start()

    def out_store(i):
        return pltpu.make_async_copy(ov.at[i], out_hbm.at[:, pl.ds(i * width, width)], qload_sem.at[i])

    def dq_store(i):
        return pltpu.make_async_copy(dqv.at[i], dq_hbm.at[:, pl.ds(i * width, width)], gload_sem.at[i])

    for i in range(groups):
        og_copy(i).wait_recv()
        for a in range(pairs):
            lanes = slice(a * 128, (a + 1) * 128)
            there = slice(width + a * 128, width + (a + 1) * 128)
            ov[i, :, lanes] = merged(mask, 0, rows, og_in[i, :, lanes], ov[i, :, lanes])
            dqv[i, :, lanes] = merged(mask, 0, rows, og_in[i, :, there], dqv[i, :, lanes])
        out_store(i).start()
        dq_store(i).start()

    dkv_copy.wait_recv()
    for pair in range(groups):
        lanes = slice(pair * 128, (pair + 1) * 128)
        dkv[:, lanes] = merged(mask, 0, rows, dkv_in[:, lanes], dkv[:, lanes])
    dk_store = pltpu.make_async_copy(dkv.at[:, pl.ds(0, kvw)], dk_hbm, store_sem.at[0])
    dv_store = pltpu.make_async_copy(dkv.at[:, pl.ds(kvw, kvw)], dv_hbm, store_sem.at[1])
    dk_store.start()
    dv_store.start()

    kv_copy.wait_send()
    diag_copy.wait_send()
    fl_copy.wait_send()
    tail_copy.wait_send()
    dkv_copy.wait_send()
    for i in range(groups):
        qg_copy(i).wait_send()
        hg_copy(i).wait_send()
        og_copy(i).wait_send()
        out_store(i).wait()
        dq_store(i).wait()
    dk_store.wait()
    dv_store.wait()


def hand_over(parts, *refs):
    count = len(parts)
    sources, targets, held = refs[:count], refs[count : 2 * count], refs[2 * count : 3 * count]
    load_sem, store_sem = refs[3 * count :]
    loads, stores = [], []
    slot = 0
    for n, cuts in enumerate(parts):
        size = sources[n].shape[0] // cuts
        for cut in range(cuts):
            at = pl.ds(cut * size, size)
            loads.append(pltpu.make_async_copy(sources[n].at[at, :], held[n].at[at, :], load_sem.at[slot]))
            stores.append(pltpu.make_async_copy(held[n].at[at, :], targets[n].at[at, :], store_sem.at[slot]))
            slot += 1
    for load in loads:
        load.start()
    for load, store in zip(loads, stores):
        load.wait()
        store.start()
    for store in stores:
        store.wait()


def shards(queries, keys, values, grad_out, sinks, doc_ids, swap_flags):
    rows = queries.shape[1]
    full = queries.shape[2]
    kvw = keys.shape[2]
    groups = KEY_VALUE_HEADS
    width = full // groups
    pairs = width // 128
    blocks = swap_flags.shape[2]
    blk = rows // blocks
    chunks = rows // WINDOW
    dims = (rows, groups, width, pairs, blocks, blk)
    vm = pltpu.VMEM
    dma = pltpu.SemaphoreType.DMA
    stack = pairs * WINDOW
    span = 4 * WINDOW
    scratch = [
        vm((rows, 2 * kvw), BF16),
        vm((groups, rows, width), BF16), vm((groups, rows, width), BF16),
        vm((chunks, stack, 128), BF16), vm((chunks, stack, 128), BF16),
        vm((groups, rows, width), BF16), vm((groups, rows, width), BF16),
        vm((rows, 2 * kvw), BF16), vm((groups, 2 * HEAD_SIZE, rows), F32),
        vm((groups, chunks, span, 128), BF16), vm((groups, chunks, span, 128), BF16),
        vm((chunks, WINDOW, 2 * WINDOW), F32), vm((rows, 128), BF16), vm((WINDOW, 128), BF16),
        vm((chunks, stack, span), F32), vm((chunks, stack, span), F32),
        vm((chunks, stack, span), BF16), vm((chunks, stack, span), BF16),
        vm((blk, 2 * kvw), BF16), vm((blk, 2 * kvw), BF16), vm((blk, 2 * kvw), BF16),
        vm((WINDOW, 2 * kvw), BF16), vm((WINDOW // blk, 128), F32), vm((WINDOW // blk, 128), F32),
        vm((groups, blk, 2 * width), BF16), vm((groups, blk, 2 * width), BF16),
        vm((groups, 2 * HEAD_SIZE, WINDOW), F32), vm((groups, 2 * HEAD_SIZE, WINDOW), F32),
        vm((groups, blk, 2 * width), BF16), vm((groups, blk, 2 * width), BF16),
        vm((blk, 2 * kvw), BF16), vm((blk, 2 * kvw), BF16),
        dma((2,)), dma((groups,)), dma((groups,)), dma((2,)),
        dma((2,)), dma((2,)), dma((2,)), dma((2,)),
        dma((groups, 2)), dma((groups, 2)), dma((groups, 2)), dma((2,)),
    ]
    hbm = pl.BlockSpec(memory_space=pl.ANY)
    smem = pl.BlockSpec(memory_space=pltpu.SMEM)
    big = jax.ShapeDtypeStruct((rows, full), BF16)
    small = jax.ShapeDtypeStruct((rows, kvw), BF16)
    results = pl.pallas_call(
        functools.partial(kernel, dims),
        out_shape=(big, big, small, small),
        in_specs=[smem, smem, pl.BlockSpec(memory_space=pltpu.VMEM), hbm, hbm, hbm, hbm],
        out_specs=(hbm, hbm, hbm, hbm),
        scratch_shapes=scratch,
        compiler_params=pltpu.CompilerParams(
            collective_id=0, has_side_effects=True, vmem_limit_bytes=65400 * 1024
        ),
        cost_estimate=pl.CostEstimate(
            flops=10 * rows * full * 2 * WINDOW, bytes_accessed=8 * rows * full, transcendentals=0
        ),
    )(swap_flags[0, 0], sinks, doc_ids, queries[0], keys[0], values[0], grad_out[0])
    parts = (4, 4, 1, 1)
    shapes = (big, big, small, small)
    results = pl.pallas_call(
        functools.partial(hand_over, parts),
        out_shape=shapes,
        in_specs=[hbm] * len(parts),
        out_specs=(hbm,) * len(parts),
        scratch_shapes=[vm(shape.shape, BF16) for shape in shapes] + [dma((sum(parts),)), dma((sum(parts),))],
        compiler_params=pltpu.CompilerParams(vmem_limit_bytes=65400 * 1024),
        cost_estimate=pl.CostEstimate(flops=0, bytes_accessed=9 * rows * full, transcendentals=0),
    )(*results)
    return tuple(result[None] for result in results)


def solution(mesh):
    rows_spec = P(("groups", "dp"), "ctx", None)
    in_specs = (rows_spec, rows_spec, rows_spec, rows_spec, P(), P(("groups", "dp"), None), rows_spec)
    return jax.shard_map(
        shards, mesh=mesh, in_specs=in_specs, out_specs=(rows_spec,) * 4, check_vma=False
    )
```
